512 devices in a mesh: py: 16 (over z_lo, x, core), pz: 32 (over y, z_hi).
Axes of the slice: x: 4, y: 8, z: 8 (z_hi: 4, z_lo: 2; z = z_hi * 2 + z_lo), core: 2. Of those that a mesh axis runs over, the one named last changes fastest.
Arguments:
- cotangent: float32 [8, 524288], P(None, ('py', 'pz')), may hold values from -6 to 6
- spline_weights: float32 [64, 524288], P(None, ('py', 'pz')), may hold values from 0 to 0.25
- base_cells: int32 [3, 524288], P(None, ('py', 'pz')), may hold values from 0 to 127, as said below
- spectral_filter: float32 [8, 128, 128, 128], P(None, 'pz', 'py'), may hold values from -3 to 6, as said below
Outputs:
- feature_grad: float32 [8, 524288], P(None, ('py', 'pz'))
The draws below stay inside these ranges and needn't reach their ends.
Inputs may be any that keep to these rules, and one draw needn't show every extreme that they name: Atom a lies in the block of the device that holds it: base_cells[0, a] // 8 * 32 + base_cells[1, a] // 4 equals a // 1024, with 32 the devices along pz. spectral_filter[c, kz, ky, kx] equals spectral_filter[c, -kz, -ky, -kx], indices taken modulo 128.
All inputs are finite; a program needn't handle non-finite values.
Results may differ from the reference program's by a relative error of at most 0.00005.
Values sent between devices are 32-bit elements; how exact they have to be, the bound alone decides.
No kernel may reach another device: no remote copies, remote signals or barrier semaphores. Data moves between devices by JAX's collectives and lax.ppermute only.
A program may use at most 128 MiB of HBM per device.

```python
import jax
import jax.numpy as jnp
from jax import lax

C = 8
MESH = 128
ATOMS_DEV = 1024
ATOMS = 524288
CX = 8
CY = 4
N_PZ = 32


def draw_base_cells(key, part):
    key = jax.random.fold_in(key, 11)
    key_x, key_y, key_z = jax.random.split(key, 3)
    device = jnp.arange(ATOMS, dtype=jnp.int32) // ATOMS_DEV
    block_x = device // N_PZ
    block_y = device % N_PZ
    inner_x = jax.random.randint(key_x, (ATOMS,), 0, CX, dtype=jnp.int32)
    inner_y = jax.random.randint(key_y, (ATOMS,), 0, CY, dtype=jnp.int32)
    cell_z = jax.random.randint(key_z, (ATOMS,), 0, MESH, dtype=jnp.int32)
    return jnp.stack([block_x * CX + inner_x, block_y * CY + inner_y, cell_z]).astype(jnp.int32)


def draw_spectral_filter(key, part):
    key = jax.random.fold_in(key, 23)
    rough = jax.random.uniform(key, (C, MESH, MESH, MESH), jnp.float32, -3.0, 3.0)
    mirror = jnp.roll(jnp.flip(rough, (1, 2, 3)), 1, (1, 2, 3))
    filt = 0.5 * (rough + mirror)
    return filt.astype(jnp.float32)


def block_levels(own_key, shape, shards, least, largest):
    def one(dim, shards_of):
        steps = jax.random.uniform(jax.random.fold_in(jax.random.fold_in(own_key, 6), dim), (shards_of,), jnp.float32, least / len(shards), largest / len(shards))
        return jnp.repeat(jnp.exp(steps), shape[dim] // shards_of).reshape((-1,) + (1,) * (len(shape) - dim - 1))

    gain = one(*shards[0])
    for cut in shards[1:]:
        gain = gain * one(*cut)
    return gain


def bell_draw(rng, shape, spread, limit, pieces=(), held_as=jnp.bfloat16):
    result = spread * jax.random.normal(rng, shape, jnp.float32)
    if pieces:
        result = result * block_levels(rng, shape, pieces, -0.22, 0.18)
    return jnp.clip(result, -limit, limit).astype(held_as)


def setup_inputs(seed: int = 0) -> dict:
    key_list = jax.random.split(jax.random.key(seed), 5)
    cotangent = bell_draw(key_list[0], (C, ATOMS), 1.0, 6.0, ((1, 512),), jnp.float32)
    spline_weights = jnp.clip(0.25 * jax.random.uniform(key_list[1], (64, ATOMS), jnp.float32) ** block_levels(key_list[1], (64, ATOMS), ((1, 512),), -0.2, 0.2), 0.0, 0.25)
    base_cells = draw_base_cells(jax.random.fold_in(key_list[4], 71), 0)
    spectral_filter = draw_spectral_filter(jax.random.fold_in(key_list[4], 71), 0)
    return {"cotangent": cotangent, "spline_weights": spline_weights, "base_cells": base_cells, "spectral_filter": spectral_filter}


def cell_of(base_cells, offset):
    step_x = offset // 16
    step_y = (offset // 4) % 4
    step_z = offset % 4
    cell_x = (base_cells[0] + step_x) % MESH
    cell_y = (base_cells[1] + step_y) % MESH
    cell_z = (base_cells[2] + step_z) % MESH
    return ((cell_x * MESH + cell_y) * MESH + cell_z).astype(jnp.int32)


def reference(cotangent, spline_weights, base_cells, spectral_filter):
    features = cotangent.T
    density = jnp.zeros((MESH * MESH * MESH, C), jnp.float32)
    for offset in range(64):
        flat = cell_of(base_cells, offset)
        density = density.at[flat].add(features * spline_weights[offset][:, None])
    density = density.reshape(MESH, MESH, MESH, C).transpose(3, 0, 1, 2)

    def convolve(pair):
        field, filt = pair
        spectrum = jnp.fft.fftn(field) * filt.transpose(2, 1, 0)
        return jnp.real(jnp.fft.ifftn(spectrum)).astype(jnp.float32)

    potential = lax.map(convolve, (density, spectral_filter)).reshape(C, -1)
    feature_grad = jnp.zeros((C, cotangent.shape[1]), jnp.float32)
    for offset in range(64):
        flat = cell_of(base_cells, offset)
        feature_grad = feature_grad + potential[:, flat] * spline_weights[offset][None, :]
    return feature_grad
```

```python
import math

import jax
import jax.numpy as jnp
import ml_dtypes
import numpy as np
from jax import lax
from jax.experimental import pallas as pl
from jax.experimental.pallas import tpu as pltpu
from jax.sharding import PartitionSpec as P

MESH = 128
CH = 8
PY = 16
PZ = 32
BX = MESH // PY
BY = MESH // PZ
EX = BX + 3
ROWS = EX * 8
LANES = 128
TILE = 128

F32 = jnp.float32
BF16 = jnp.bfloat16


def halves(table):
    high = table.astype(ml_dtypes.bfloat16)
    low = (table - high.astype(np.float64)).astype(ml_dtypes.bfloat16)
    return high, low


def turn(numerator, denominator):
    angle = 2.0 * math.pi * (numerator % denominator) / denominator
    return np.cos(angle) + 1j * np.sin(angle)


def z_tables():
    z = np.arange(MESH)
    forth = np.zeros((2, PZ, 2, MESH))
    back = np.zeros((2, PZ, 2, MESH))
    scale = 1.0 / float(MESH) ** 3
    for s in range(2):
        for q in range(PZ):
            kz = 4 * q + s + (1 if q >= PZ // 2 else 0)
            wave = turn(kz * z, MESH)
            forth[s, q, 0] = wave.real
            forth[s, q, 1] = -wave.imag
            back[s, q, 0] = 2.0 * scale * wave.real
            back[s, q, 1] = -2.0 * scale * wave.imag
    sign = 1.0 - 2.0 * (z % 2)
    forth[0, 0, 0] = 1.0
    forth[0, 0, 1] = sign
    back[0, 0, 0] = scale
    back[0, 0, 1] = scale * sign
    return forth.reshape(128, MESH), back.reshape(128, MESH)


def plane_tables():
    k0 = np.arange(PZ)
    wave = turn(-np.outer(k0, np.arange(PZ)), PZ)
    first = np.zeros((2, PZ, PZ, 2))
    first[0, :, :, 0] = wave.real
    first[0, :, :, 1] = -wave.imag
    first[1, :, :, 0] = wave.imag
    first[1, :, :, 1] = wave.real
    first = np.kron(np.eye(4), first.reshape(64, 64))
    xl = np.zeros(LANES, np.int64)
    yl = np.zeros(LANES, np.int64)
    used = np.zeros(LANES)
    for x in range(EX):
        for y in range(BY + 3):
            xl[8 * x + y] = x
            yl[8 * x + y] = y
            used[8 * x + y] = 1.0
    kx0 = np.repeat(np.arange(PY), PZ)
    ky0 = np.tile(np.arange(PZ), PY)
    twist = turn(-(kx0[:, None] * xl[None] + ky0[:, None] * yl[None]), MESH) * used
    m = np.repeat(np.arange(8), 4)
    n = np.tile(np.arange(4), 8)
    fine = turn(-(4 * m[None] * xl[:, None] + 8 * n[None] * yl[:, None]), 32) * used[:, None]
    second = np.zeros((2, LANES, 2, 2, 32))
    for ab in range(2):
        second[0, :, ab, 0] = fine.real
        second[1, :, ab, 0] = -fine.imag
        second[0, :, ab, 1] = fine.imag
        second[1, :, ab, 1] = fine.real
    third = np.zeros((2, 2, 32, 2, 2, LANES))
    for ab in range(2):
        third[ab, 0, :, ab, 0] = fine.real.T
        third[ab, 1, :, ab, 0] = fine.imag.T
        third[ab, 0, :, ab, 1] = -fine.imag.T
        third[ab, 1, :, ab, 1] = fine.real.T
    last = np.zeros((PZ, 2, 2, 2, PZ))
    last[:, 0, 0, 0] = wave.real.T
    last[:, 0, 0, 1] = wave.imag.T
    last[:, 1, 1, 0] = -wave.imag.T
    last[:, 1, 1, 1] = wave.real.T
    last = np.kron(np.eye(2), last.reshape(64, 128))
    twist = np.stack([twist.real, twist.imag]).astype(np.float32)
    return first, twist, second.reshape(256, 128), third.reshape(128, 512), last


def split(value):
    high = value.astype(BF16)
    return high, (value - high.astype(F32)).astype(BF16)


def mm(a, b, dims=((1,), (0,))):
    return lax.dot_general(a, b, (dims, ((), ())), preferred_element_type=F32)


def fft4(x, sign):
    (ar, ai), (br, bi), (cr, ci), (dr, di) = x
    sr, si, tr, ti = ar + cr, ai + ci, ar - cr, ai - ci
    ur, ui, vr, vi = br + dr, bi + di, br - dr, bi - di
    if sign < 0:
        return [(sr + ur, si + ui), (tr + vi, ti - vr), (sr - ur, si - ui), (tr - vi, ti + vr)]
    return [(sr + ur, si + ui), (tr - vi, ti + vr), (sr - ur, si - ui), (tr + vi, ti - vr)]


def times(value, k, sign):
    re, im = value
    k %= 16
    if k == 0:
        return value
    if k == 4:
        return (-sign * im, sign * re)
    c, s = math.cos(2.0 * math.pi * k / 16), sign * math.sin(2.0 * math.pi * k / 16)
    if k in (2, 6):
        h = math.sqrt(0.5)
        if k == 2:
            return ((re - sign * im) * h, (im + sign * re) * h)
        return ((re + sign * im) * -h, (sign * re - im) * h)
    return (re * c - im * s, im * c + re * s)


def fft16(x, sign):
    inner = [fft4([x[4 * a + b] for a in range(4)], sign) for b in range(4)]
    out = [None] * 16
    for k in range(4):
        column = fft4([times(inner[b][k], b * k, sign) for b in range(4)], sign)
        for a in range(4):
            out[k + 4 * a] = column[a]
    return out


def atom_weights(w_ref, cells_ref, lo):
    at = slice(lo, lo + TILE)
    lx = cells_ref[0:1, at] & (BX - 1)
    ly = cells_ref[1:2, at] & (BY - 1)
    lx = jnp.broadcast_to(lx, (8, TILE))
    dy = lax.broadcasted_iota(jnp.int32, (8, TILE), 0) - ly
    on_y = [dy == j for j in range(4)]
    on_x = [lx == x for x in range(BX)]
    zero = jnp.zeros((8, TILE), F32)
    rows = [[None] * 4 for _ in range(4)]
    for i in range(4):
        for k in range(4):
            value = zero
            for j in range(4):
                row = jnp.broadcast_to(w_ref[16 * i + 4 * j + k : 16 * i + 4 * j + k + 1, at], (8, TILE))
                value = jnp.where(on_y[j], row, value)
            rows[i][k] = value
    spread = [[None] * 4 for _ in range(EX)]
    for x in range(EX):
        for k in range(4):
            value = zero
            for i in range(4):
                if 0 <= x - i < BX:
                    value = jnp.where(on_x[x - i], rows[i][k], value)
            spread[x][k] = value
    return spread


def z_hits(cells_ref, lo, k):
    bz = cells_ref[2:3, lo : lo + TILE]
    z = lax.broadcasted_iota(jnp.int32, (MESH, TILE), 0)
    return jnp.where(z == ((bz + k) & (MESH - 1)), 1.0, 0.0).astype(BF16)


def scatter_kernel(cot_ref, w_ref, cells_ref, mh_ref, ml_ref, out_ref, gh_ref, gl_ref, hit_ref, den_ref):
    atoms = cot_ref.shape[1]
    for t in range(atoms // TILE):
        lo = t * TILE
        slot = t % 2
        spread = atom_weights(w_ref, cells_ref, lo)
        for k in range(4):
            hit_ref[slot, :, k * TILE : (k + 1) * TILE] = z_hits(cells_ref, lo, k)
        for c in range(0, CH, 2):
            cots = [jnp.broadcast_to(cot_ref[c + h : c + h + 1, lo : lo + TILE], (8, TILE)) for h in range(2)]
            for k in range(4):
                g = jnp.concatenate([spread[x][k] * cots[h] for h in range(2) for x in range(EX)], axis=0)
                high, low = split(g)
                gh_ref[slot, c * ROWS : (c + 2) * ROWS, k * TILE : (k + 1) * TILE] = high
                gl_ref[slot, c * ROWS : (c + 2) * ROWS, k * TILE : (k + 1) * TILE] = low
        hit = hit_ref[slot]
        part = mm(gh_ref[slot], hit, ((1,), (1,))) + mm(gl_ref[slot], hit, ((1,), (1,)))
        if t == 0:
            den_ref[...] = part
        else:
            den_ref[...] += part
    for c in range(CH):
        rows = jnp.concatenate([den_ref[c * ROWS : (c + 1) * ROWS, :], jnp.zeros((LANES - ROWS, MESH), F32)], axis=0)
        high, low = split(rows)
        nt = ((1,), (1,))
        out_ref[c * 128 : (c + 1) * 128, :] = (
            mm(mh_ref[...], high, nt) + mm(ml_ref[...], high, nt) + mm(mh_ref[...], low, nt)
        )


def plane_kernel(in_ref, filt_ref, fh_ref, fl_ref, tw_ref, sh_ref, sl_ref, th_ref, tl_ref, lh_ref, ll_ref, out_ref):
    rows = []
    for p4 in range(PY // 4):
        high, low = split(in_ref[256 * p4 : 256 * (p4 + 1), :])
        part = mm(fh_ref[...], high) + mm(fl_ref[...], high) + mm(fh_ref[...], low)
        for p in range(4):
            rows.append((part[64 * p : 64 * p + 32], part[64 * p + 32 : 64 * p + 64]))
    rows = fft16(rows, -1)
    turned = []
    for k in range(PY):
        at = slice(PZ * k, PZ * (k + 1))
        tr, ti = tw_ref[0, at, :], tw_ref[1, at, :]
        re, im = rows[k]
        turned.append(jnp.concatenate([re * tr - im * ti, im * tr + re * ti], axis=1))
    high, low = split(jnp.concatenate(turned, axis=0))
    spec = mm(high, sh_ref[...]) + mm(high, sl_ref[...]) + mm(low, sh_ref[...])
    high, low = split(spec * filt_ref[...])
    both = mm(high, th_ref[...]) + mm(high, tl_ref[...]) + mm(low, th_ref[...])
    back = []
    for k in range(PY):
        at = slice(PZ * k, PZ * (k + 1))
        tr, ti = tw_ref[0, at, :], tw_ref[1, at, :]
        cols = []
        for ab in range(2):
            re, im = both[at, 256 * ab : 256 * ab + 128], both[at, 256 * ab + 128 : 256 * ab + 256]
            cols.append((re * tr + im * ti, im * tr - re * ti))
        back.append(cols)
    a = fft16([cols[0] for cols in back], 1)
    b = fft16([cols[1] for cols in back], 1)
    for p in range(0, PY, 2):
        stack = jnp.concatenate([a[p][0], a[p][1], b[p][0], b[p][1], a[p + 1][0], a[p + 1][1], b[p + 1][0], b[p + 1][1]], axis=0)
        high, low = split(stack)
        out_ref[64 * p : 64 * (p + 2), :] = mm(lh_ref[...], high) + mm(ll_ref[...], high) + mm(lh_ref[...], low)


def gather_kernel(in_ref, w_ref, cells_ref, bh_ref, bl_ref, out_ref, pot_ref, hit_ref, near_ref):
    atoms = out_ref.shape[1]
    for c in range(0, CH, 2):
        pots = []
        for h in range(2):
            high, low = split(in_ref[(c + h) * 128 : (c + h + 1) * 128, :].T)
            pot = mm(high, bh_ref[...]) + mm(high, bl_ref[...]) + mm(low, bh_ref[...])
            pots.append(pot[:ROWS])
        high, low = split(jnp.concatenate(pots, axis=0))
        pot_ref[c * ROWS : (c + 2) * ROWS, 0:MESH] = high
        pot_ref[c * ROWS : (c + 2) * ROWS, MESH : 2 * MESH] = low
    for t in range(atoms // TILE):
        lo = t * TILE
        slot = t % 2
        spread = atom_weights(w_ref, cells_ref, lo)
        for k in range(4):
            hit = z_hits(cells_ref, lo, k)
            hit_ref[slot, 0:MESH, k * TILE : (k + 1) * TILE] = hit
            hit_ref[slot, MESH : 2 * MESH, k * TILE : (k + 1) * TILE] = hit
        near_ref[slot] = mm(pot_ref[...], hit_ref[slot])
        for c in range(CH):
            total = jnp.zeros((8, TILE), F32)
            for x in range(EX):
                for k in range(4):
                    r = c * ROWS + 8 * x
                    total = total + spread[x][k] * near_ref[slot, r : r + 8, k * TILE : (k + 1) * TILE]
            out_ref[c : c + 1, lo : lo + TILE] = jnp.sum(total, axis=0, keepdims=True)


VMEM = pl.BlockSpec(memory_space=pltpu.VMEM)


def call(kernel, out_shape, scratch, flops, moved, *args):
    return pl.pallas_call(
        kernel,
        out_shape=jax.ShapeDtypeStruct(out_shape, F32),
        in_specs=[VMEM] * len(args),
        out_specs=VMEM,
        scratch_shapes=scratch,
        compiler_params=pltpu.CompilerParams(vmem_limit_bytes=40 * 1024 * 1024),
        cost_estimate=pl.CostEstimate(flops=flops, bytes_accessed=moved, transcendentals=0),
    )(*args)


def scatter(cotangent, spline_weights, base_cells):
    forth, _ = z_tables()
    scratch = [
        pltpu.VMEM((2, CH * ROWS, 4 * TILE), BF16),
        pltpu.VMEM((2, CH * ROWS, 4 * TILE), BF16),
        pltpu.VMEM((2, MESH, 4 * TILE), BF16),
        pltpu.VMEM((CH * ROWS, MESH), F32),
    ]
    return call(scatter_kernel, (CH * 128, LANES), scratch, 3 * 10**9, 10**6, cotangent, spline_weights, base_cells, *halves(forth))


def plane(blocks, filt):
    first, twist, second, third, last = plane_tables()
    return call(
        plane_kernel, (PY * PZ * 2, LANES), [], 10**9, 2 * 10**6,
        blocks, filt, *halves(first), twist, *halves(second), *halves(third), *halves(last),
    )


def gather(blocks, spline_weights, base_cells):
    _, back = z_tables()
    atoms = spline_weights.shape[1]
    scratch = [
        pltpu.VMEM((CH * ROWS, 2 * MESH), BF16),
        pltpu.VMEM((2, 2 * MESH, 4 * TILE), BF16),
        pltpu.VMEM((2, CH * ROWS, 4 * TILE), F32),
    ]
    return call(gather_kernel, (CH, atoms), scratch, 3 * 10**9, 10**6, blocks, spline_weights, base_cells, *halves(back))


def plane_filter(spectral_filter):
    q = lax.axis_index("pz")
    half = PZ // 2
    mine = jnp.where(q >= half, spectral_filter[:, 1:3], spectral_filter[:, 0:2])
    top = lax.ppermute(spectral_filter[:, 0], "pz", [(half, 0)])
    other = jnp.where(q == 0, top, mine[:, 0])
    other = jnp.stack([other, mine[:, 1]], axis=1)
    both = jnp.stack([mine, other], axis=2).reshape(PY, 2, BX, MESH)
    both = lax.all_to_all(both, "py", 0, 0)
    both = both.reshape(4, 4, 2, 8, 8, 16).transpose(5, 1, 3, 2, 4, 0).reshape(PY * PZ, 2, 1, 32)
    return jnp.broadcast_to(both, (PY * PZ, 2, 2, 32)).reshape(PY * PZ, 128)


def exchange(blocks):
    return lax.all_to_all(blocks.reshape(PY * PZ, 2, LANES), ("py", "pz"), 0, 0).reshape(PY * PZ * 2, LANES)


def on_device(cotangent, spline_weights, base_cells, spectral_filter):
    filt = plane_filter(spectral_filter)
    blocks = scatter(cotangent, spline_weights, base_cells)
    blocks = exchange(blocks)
    blocks = plane(blocks, filt)
    blocks = exchange(blocks)
    return gather(blocks, spline_weights, base_cells)


def solution(mesh):
    return jax.shard_map(
        on_device,
        mesh=mesh,
        in_specs=(
            P(None, ("py", "pz")),
            P(None, ("py", "pz")),
            P(None, ("py", "pz")),
            P(None, "pz", "py", None),
        ),
        out_specs=P(None, ("py", "pz")),
        check_vma=False,
    )
```

```python
import math

import jax
import jax.numpy as jnp
import ml_dtypes
import numpy as np
from jax import lax
from jax.experimental import pallas as pl
from jax.experimental.pallas import tpu as pltpu
from jax.sharding import PartitionSpec as P

MESH = 128
CH = 8
PY = 16
PZ = 32
BX = MESH // PY
BY = MESH // PZ
EX = BX + 3
ROWS = EX * 8
LANES = 128
TILE = 128

F32 = jnp.float32
BF16 = jnp.bfloat16


def halves(table):
    high = table.astype(ml_dtypes.bfloat16)
    low = (table - high.astype(np.float64)).astype(ml_dtypes.bfloat16)
    return high, low


def turn(numerator, denominator):
    angle = 2.0 * math.pi * (numerator % denominator) / denominator
    return np.cos(angle) + 1j * np.sin(angle)


def z_tables():
    z = np.arange(MESH)
    forth = np.zeros((2, PZ, 2, MESH))
    back = np.zeros((2, PZ, 2, MESH))
    scale = 1.0 / float(MESH) ** 3
    for s in range(2):
        for q in range(PZ):
            kz = 4 * q + 2 * s + (1 if q < PZ // 2 else 0)
            wave = turn(kz * z, MESH)
            forth[s, q, 0] = wave.real
            forth[s, q, 1] = -wave.imag
            back[s, q, 0] = 2.0 * scale * wave.real
            back[s, q, 1] = -2.0 * scale * wave.imag
    sign = 1.0 - 2.0 * (z % 2)
    forth[0, PZ // 2, 0] = 1.0
    forth[0, PZ // 2, 1] = sign
    back[0, PZ // 2, 0] = scale
    back[0, PZ // 2, 1] = scale * sign
    return forth.reshape(128, MESH), back.reshape(128, MESH)


def plane_tables():
    k0 = np.arange(PZ)
    wave = turn(-np.outer(k0, np.arange(PZ)), PZ)
    first = np.zeros((2, PZ, PZ, 2))
    first[0, :, :, 0] = wave.real
    first[0, :, :, 1] = -wave.imag
    first[1, :, :, 0] = wave.imag
    first[1, :, :, 1] = wave.real
    first = np.kron(np.eye(4), first.reshape(64, 64))
    xl = np.zeros(LANES, np.int64)
    yl = np.zeros(LANES, np.int64)
    used = np.zeros(LANES)
    for x in range(EX):
        for y in range(BY + 3):
            xl[8 * x + y] = x
            yl[8 * x + y] = y
            used[8 * x + y] = 1.0
    kx0 = np.repeat(np.arange(PY), PZ)
    ky0 = np.tile(np.arange(PZ), PY)
    twist = turn(-(kx0[:, None] * xl[None] + ky0[:, None] * yl[None]), MESH) * used
    m = np.repeat(np.arange(8), 4)
    n = np.tile(np.arange(4), 8)
    fine = turn(-(4 * m[None] * xl[:, None] + 8 * n[None] * yl[:, None]), 32) * used[:, None]
    second = np.zeros((2, LANES, 2, 2, 32))
    for ab in range(2):
        second[0, :, ab, 0] = fine.real
        second[1, :, ab, 0] = -fine.imag
        second[0, :, ab, 1] = fine.imag
        second[1, :, ab, 1] = fine.real
    third = np.zeros((2, 2, 32, 2, 2, LANES))
    for ab in range(2):
        third[ab, 0, :, ab, 0] = fine.real.T
        third[ab, 1, :, ab, 0] = fine.imag.T
        third[ab, 0, :, ab, 1] = -fine.imag.T
        third[ab, 1, :, ab, 1] = fine.real.T
    last = np.zeros((PZ, 2, 2, 2, PZ))
    last[:, 0, 0, 0] = wave.real.T
    last[:, 0, 0, 1] = wave.imag.T
    last[:, 1, 1, 0] = -wave.imag.T
    last[:, 1, 1, 1] = wave.real.T
    last = np.kron(np.eye(2), last.reshape(64, 128))
    twist = np.stack([twist.real, twist.imag]).astype(np.float32)
    return first, twist, second.reshape(256, 128), third.reshape(128, 512), last


def split(value):
    high = value.astype(BF16)
    return high, (value - high.astype(F32)).astype(BF16)


def mm(a, b, dims=((1,), (0,))):
    return lax.dot_general(a, b, (dims, ((), ())), preferred_element_type=F32)


def fft4(x, sign):
    (ar, ai), (br, bi), (cr, ci), (dr, di) = x
    sr, si, tr, ti = ar + cr, ai + ci, ar - cr, ai - ci
    ur, ui, vr, vi = br + dr, bi + di, br - dr, bi - di
    if sign < 0:
        return [(sr + ur, si + ui), (tr + vi, ti - vr), (sr - ur, si - ui), (tr - vi, ti + vr)]
    return [(sr + ur, si + ui), (tr - vi, ti + vr), (sr - ur, si - ui), (tr + vi, ti - vr)]


def times(value, k, sign):
    re, im = value
    k %= 16
    if k == 0:
        return value
    if k == 4:
        return (-sign * im, sign * re)
    c, s = math.cos(2.0 * math.pi * k / 16), sign * math.sin(2.0 * math.pi * k / 16)
    if k in (2, 6):
        h = math.sqrt(0.5)
        if k == 2:
            return ((re - sign * im) * h, (im + sign * re) * h)
        return ((re + sign * im) * -h, (sign * re - im) * h)
    return (re * c - im * s, im * c + re * s)


def fft16(x, sign):
    inner = [fft4([x[4 * a + b] for a in range(4)], sign) for b in range(4)]
    out = [None] * 16
    for k in range(4):
        column = fft4([times(inner[b][k], b * k, sign) for b in range(4)], sign)
        for a in range(4):
            out[k + 4 * a] = column[a]
    return out


def atom_weights(w_ref, cells_ref, lo):
    at = slice(lo, lo + TILE)
    lx = cells_ref[0:1, at] & (BX - 1)
    ly = cells_ref[1:2, at] & (BY - 1)
    lx = jnp.broadcast_to(lx, (8, TILE))
    dy = lax.broadcasted_iota(jnp.int32, (8, TILE), 0) - ly
    on_y = [dy == j for j in range(4)]
    on_x = [lx == x for x in range(BX)]
    zero = jnp.zeros((8, TILE), F32)
    rows = [[None] * 4 for _ in range(4)]
    for i in range(4):
        for k in range(4):
            value = zero
            for j in range(4):
                row = jnp.broadcast_to(w_ref[16 * i + 4 * j + k : 16 * i + 4 * j + k + 1, at], (8, TILE))
                value = jnp.where(on_y[j], row, value)
            rows[i][k] = value
    spread = [[None] * 4 for _ in range(EX)]
    for x in range(EX):
        for k in range(4):
            value = zero
            for i in range(4):
                if 0 <= x - i < BX:
                    value = jnp.where(on_x[x - i], rows[i][k], value)
            spread[x][k] = value
    return spread


def z_hits(cells_ref, lo, k):
    bz = cells_ref[2:3, lo : lo + TILE]
    z = lax.broadcasted_iota(jnp.int32, (MESH, TILE), 0)
    return jnp.where(z == ((bz + k) & (MESH - 1)), 1.0, 0.0).astype(BF16)


def scatter_kernel(cot_in, w_in, cells_in, m_in, out_ref, cot_ref, w_ref, cells_ref, m_ref, hit_ref, den_ref, sems):
    pairs = ((cells_in, cells_ref), (cot_in, cot_ref), (w_in, w_ref), (m_in, m_ref))
    copies = [pltpu.make_async_copy(a, b, sems.at[i]) for i, (a, b) in enumerate(pairs)]
    for copy in copies:
        copy.start()
    for copy in copies[:3]:
        copy.wait()
    atoms = cot_ref.shape[1]
    for t in range(atoms // TILE):
        lo = t * TILE
        slot = t % 2
        spread = atom_weights(w_ref, cells_ref, lo)
        bz = jnp.broadcast_to(cells_ref[2:3, lo : lo + TILE], (TILE, TILE)).T
        zz = lax.broadcasted_iota(jnp.int32, (TILE, MESH), 1)
        for k in range(4):
            hit_ref[slot, k * TILE : (k + 1) * TILE, :] = jnp.where(zz == ((bz + k) & (MESH - 1)), 1.0, 0.0).astype(BF16)
        hit = hit_ref[slot]
        for c in range(0, CH, 2):
            cots = [jnp.broadcast_to(cot_ref[c + h : c + h + 1, lo : lo + TILE], (8, TILE)) for h in range(2)]
            hs, ls = [], []
            for k in range(4):
                g = jnp.concatenate([spread[x][k] * cots[h] for h in range(2) for x in range(EX)], axis=0)
                high, low = split(g)
                hs.append(high)
                ls.append(low)
            part = mm(jnp.concatenate(hs, axis=1), hit) + mm(jnp.concatenate(ls, axis=1), hit)
            at = slice(c * ROWS, (c + 2) * ROWS)
            if t == 0:
                den_ref[at, :] = part
            else:
                den_ref[at, :] += part
    copies[3].wait()
    mh, ml = m_ref[0], m_ref[1]
    for c in range(CH):
        rows = jnp.concatenate([den_ref[c * ROWS : (c + 1) * ROWS, :], jnp.zeros((LANES - ROWS, MESH), F32)], axis=0)
        high, low = split(rows)
        nt = ((1,), (1,))
        out_ref[c * 128 : (c + 1) * 128, :] = (
            mm(mh, high, nt) + mm(ml, high, nt) + mm(mh, low, nt)
        )


def plane_kernel(in_ref, filt_ref, fh_ref, fl_ref, tw_ref, sh_ref, sl_ref, th_ref, tl_ref, lh_ref, ll_ref, out_ref):
    rows = []
    for p4 in range(PY // 4):
        high, low = split(in_ref[256 * p4 : 256 * (p4 + 1), :])
        part = mm(fh_ref[...], high) + mm(fl_ref[...], high) + mm(fh_ref[...], low)
        for p in range(4):
            rows.append((part[64 * p : 64 * p + 32], part[64 * p + 32 : 64 * p + 64]))
    rows = fft16(rows, -1)
    turned = []
    for k in range(PY):
        at = slice(PZ * k, PZ * (k + 1))
        tr, ti = tw_ref[0, at, :], tw_ref[1, at, :]
        re, im = rows[k]
        turned.append(jnp.concatenate([re * tr - im * ti, im * tr + re * ti], axis=1))
    high, low = split(jnp.concatenate(turned, axis=0))
    spec = mm(high, sh_ref[...]) + mm(high, sl_ref[...]) + mm(low, sh_ref[...])
    high, low = split(spec * filt_ref[...])
    both = mm(high, th_ref[...]) + mm(high, tl_ref[...]) + mm(low, th_ref[...])
    back = []
    for k in range(PY):
        at = slice(PZ * k, PZ * (k + 1))
        tr, ti = tw_ref[0, at, :], tw_ref[1, at, :]
        cols = []
        for ab in range(2):
            re, im = both[at, 256 * ab : 256 * ab + 128], both[at, 256 * ab + 128 : 256 * ab + 256]
            cols.append((re * tr + im * ti, im * tr - re * ti))
        back.append(cols)
    a = fft16([cols[0] for cols in back], 1)
    b = fft16([cols[1] for cols in back], 1)
    for p in range(0, PY, 2):
        stack = jnp.concatenate([a[p][0], a[p][1], b[p][0], b[p][1], a[p + 1][0], a[p + 1][1], b[p + 1][0], b[p + 1][1]], axis=0)
        high, low = split(stack)
        out_ref[64 * p : 64 * (p + 2), :] = mm(lh_ref[...], high) + mm(ll_ref[...], high) + mm(lh_ref[...], low)


def gather_kernel(in_ref, w_ref, cells_ref, bh_ref, bl_ref, out_ref, pot_ref, hit_ref, near_ref):
    atoms = out_ref.shape[1]
    for c in range(0, CH, 2):
        pots = []
        for h in range(2):
            high, low = split(in_ref[(c + h) * 128 : (c + h + 1) * 128, :].T)
            pot = mm(high, bh_ref[...]) + mm(high, bl_ref[...]) + mm(low, bh_ref[...])
            pots.append(pot[:ROWS])
        high, low = split(jnp.concatenate(pots, axis=0))
        pot_ref[c * ROWS : (c + 2) * ROWS, 0:MESH] = high
        pot_ref[c * ROWS : (c + 2) * ROWS, MESH : 2 * MESH] = low
    for t in range(atoms // TILE):
        lo = t * TILE
        slot = t % 2
        spread = atom_weights(w_ref, cells_ref, lo)
        for k in range(4):
            hit = z_hits(cells_ref, lo, k)
            hit_ref[slot, 0:MESH, k * TILE : (k + 1) * TILE] = hit
            hit_ref[slot, MESH : 2 * MESH, k * TILE : (k + 1) * TILE] = hit
        near_ref[slot] = mm(pot_ref[...], hit_ref[slot])
        for c in range(CH):
            total = jnp.zeros((8, TILE), F32)
            for x in range(EX):
                for k in range(4):
                    r = c * ROWS + 8 * x
                    total = total + spread[x][k] * near_ref[slot, r : r + 8, k * TILE : (k + 1) * TILE]
            out_ref[c : c + 1, lo : lo + TILE] = jnp.sum(total, axis=0, keepdims=True)


def call(kernel, out_shape, scratch, flops, moved, *args, space=pltpu.VMEM, limit=40):
    return pl.pallas_call(
        kernel,
        out_shape=jax.ShapeDtypeStruct(out_shape, F32),
        in_specs=[pl.BlockSpec(memory_space=space)] * len(args),
        out_specs=pl.BlockSpec(memory_space=pltpu.VMEM),
        scratch_shapes=scratch,
        compiler_params=pltpu.CompilerParams(vmem_limit_bytes=limit * 1024 * 1024),
        cost_estimate=pl.CostEstimate(flops=flops, bytes_accessed=moved, transcendentals=0),
    )(*args)


def scatter(cotangent, spline_weights, base_cells):
    forth, _ = z_tables()
    table = np.stack(halves(forth))
    args = (cotangent, spline_weights, base_cells, table)
    scratch = [pltpu.VMEM(a.shape, a.dtype) for a in args] + [
        pltpu.VMEM((2, 4 * TILE, MESH), BF16),
        pltpu.VMEM((CH * ROWS, MESH), F32),
        pltpu.SemaphoreType.DMA((4,)),
    ]
    return call(scatter_kernel, (CH * 128, LANES), scratch, 3 * 10**9, 10**6, *args, space=pltpu.HBM, limit=60)


def plane(blocks, filt):
    first, twist, second, third, last = plane_tables()
    return call(
        plane_kernel, (PY * PZ * 2, LANES), [], 10**9, 2 * 10**6,
        blocks, filt, *halves(first), twist, *halves(second), *halves(third), *halves(last),
    )


def gather(blocks, spline_weights, base_cells):
    _, back = z_tables()
    atoms = spline_weights.shape[1]
    scratch = [
        pltpu.VMEM((CH * ROWS, 2 * MESH), BF16),
        pltpu.VMEM((2, 2 * MESH, 4 * TILE), BF16),
        pltpu.VMEM((2, CH * ROWS, 4 * TILE), F32),
    ]
    return call(gather_kernel, (CH, atoms), scratch, 3 * 10**9, 10**6, blocks, spline_weights, base_cells, *halves(back))


def plane_filter(spectral_filter):
    p, q = lax.axis_index("py"), lax.axis_index("pz")
    half = PZ // 2
    pair = lax.all_to_all(spectral_filter.reshape(PY, 2, BX, MESH), "py", 0, 0)
    even = lax.ppermute(pair[:, 0], "pz", [(0, half)])
    mine = jnp.where(q < half, pair[:, 1], pair[:, 0])
    shared = (q == half) & (p % 2 == 0)
    both = jnp.stack([jnp.where(shared, even, mine), mine], axis=1)
    both = both.reshape(4, 4, 2, 8, 8, 16).transpose(5, 1, 3, 2, 4, 0).reshape(PY * PZ, 2, 1, 32)
    return jnp.broadcast_to(both, (PY * PZ, 2, 2, 32)).reshape(PY * PZ, 128)


def exchange(blocks):
    return lax.all_to_all(blocks.reshape(PY * PZ, 2, LANES), ("py", "pz"), 0, 0).reshape(PY * PZ * 2, LANES)


def on_device(cotangent, spline_weights, base_cells, spectral_filter):
    filt = plane_filter(spectral_filter)
    blocks = scatter(cotangent, spline_weights, base_cells)
    blocks = exchange(blocks)
    blocks = plane(blocks, filt)
    blocks = exchange(blocks)
    return gather(blocks, spline_weights, base_cells)


def solution(mesh):
    return jax.shard_map(
        on_device,
        mesh=mesh,
        in_specs=(
            P(None, ("py", "pz")),
            P(None, ("py", "pz")),
            P(None, ("py", "pz")),
            P(None, "pz", "py", None),
        ),
        out_specs=P(None, ("py", "pz")),
        check_vma=False,
    )
```

```python
import math

import jax
import jax.numpy as jnp
import ml_dtypes
import numpy as np
from jax import lax
from jax.experimental import pallas as pl
from jax.experimental.pallas import tpu as pltpu
from jax.sharding import PartitionSpec as P

MESH = 128
CH = 8
PY = 16
PZ = 32
BX = MESH // PY
BY = MESH // PZ
EX = BX + 3
ROWS = EX * 8
LANES = 128
TILE = 128

F32 = jnp.float32
BF16 = jnp.bfloat16


def halves(table):
    high = table.astype(ml_dtypes.bfloat16)
    low = (table - high.astype(np.float64)).astype(ml_dtypes.bfloat16)
    return high, low


def turn(numerator, denominator):
    angle = 2.0 * math.pi * (numerator % denominator) / denominator
    return np.cos(angle) + 1j * np.sin(angle)


def z_tables():
    z = np.arange(MESH)
    forth = np.zeros((2, PZ, 2, MESH))
    back = np.zeros((2, PZ, 2, MESH))
    scale = 1.0 / float(MESH) ** 3
    for s in range(2):
        for q in range(PZ):
            kz = 4 * q + 2 * s + (1 if q < PZ // 2 else 0)
            wave = turn(kz * z, MESH)
            forth[s, q, 0] = wave.real
            forth[s, q, 1] = -wave.imag
            back[s, q, 0] = 2.0 * scale * wave.real
            back[s, q, 1] = -2.0 * scale * wave.imag
    sign = 1.0 - 2.0 * (z % 2)
    forth[0, PZ // 2, 0] = 1.0
    forth[0, PZ // 2, 1] = sign
    back[0, PZ // 2, 0] = scale
    back[0, PZ // 2, 1] = scale * sign
    return forth.reshape(128, MESH), back.reshape(128, MESH)


def plane_tables():
    k0 = np.arange(PZ)
    wave = turn(-np.outer(k0, np.arange(PZ)), PZ)
    first = np.zeros((2, PZ, PZ, 2))
    first[0, :, :, 0] = wave.real
    first[0, :, :, 1] = -wave.imag
    first[1, :, :, 0] = wave.imag
    first[1, :, :, 1] = wave.real
    first = np.kron(np.eye(4), first.reshape(64, 64))
    xl = np.zeros(LANES, np.int64)
    yl = np.zeros(LANES, np.int64)
    used = np.zeros(LANES)
    for x in range(EX):
        for y in range(BY + 3):
            xl[8 * x + y] = x
            yl[8 * x + y] = y
            used[8 * x + y] = 1.0
    kx0 = np.repeat(np.arange(PY), PZ)
    ky0 = np.tile(np.arange(PZ), PY)
    twist = turn(-(kx0[:, None] * xl[None] + ky0[:, None] * yl[None]), MESH) * used
    m = np.repeat(np.arange(8), 4)
    n = np.tile(np.arange(4), 8)
    fine = turn(-(4 * m[None] * xl[:, None] + 8 * n[None] * yl[:, None]), 32) * used[:, None]
    second = np.zeros((2, LANES, 4, 2, 32))
    second[0, :, :, 0] = fine.real[:, None]
    second[1, :, :, 0] = -fine.imag[:, None]
    second[0, :, :, 1] = fine.imag[:, None]
    second[1, :, :, 1] = fine.real[:, None]
    third = np.zeros((2, 32, 2, LANES))
    third[0, :, 0] = fine.real.T
    third[1, :, 0] = fine.imag.T
    third[0, :, 1] = -fine.imag.T
    third[1, :, 1] = fine.real.T
    high, low = halves(third.reshape(64, 256))
    third = np.concatenate([high, low, high, low])
    last = np.zeros((PZ, 2, 2, 2, PZ))
    last[:, 0, 0, 0] = wave.real.T
    last[:, 0, 0, 1] = wave.imag.T
    last[:, 1, 1, 0] = -wave.imag.T
    last[:, 1, 1, 1] = wave.real.T
    last = np.kron(np.eye(2), last.reshape(64, 128))
    twist = np.stack([twist.real, twist.imag]).astype(np.float32)
    return first, twist, second.reshape(256, 256), third, last


def split(value):
    high = value.astype(BF16)
    return high, (value - high.astype(F32)).astype(BF16)


def mm(a, b, dims=((1,), (0,))):
    return lax.dot_general(a, b, (dims, ((), ())), preferred_element_type=F32)


def fft4(x, sign):
    (ar, ai), (br, bi), (cr, ci), (dr, di) = x
    sr, si, tr, ti = ar + cr, ai + ci, ar - cr, ai - ci
    ur, ui, vr, vi = br + dr, bi + di, br - dr, bi - di
    if sign < 0:
        return [(sr + ur, si + ui), (tr + vi, ti - vr), (sr - ur, si - ui), (tr - vi, ti + vr)]
    return [(sr + ur, si + ui), (tr - vi, ti + vr), (sr - ur, si - ui), (tr + vi, ti - vr)]


def times(value, k, sign):
    re, im = value
    k %= 16
    if k == 0:
        return value
    if k == 4:
        return (-sign * im, sign * re)
    c, s = math.cos(2.0 * math.pi * k / 16), sign * math.sin(2.0 * math.pi * k / 16)
    if k in (2, 6):
        h = math.sqrt(0.5)
        if k == 2:
            return ((re - sign * im) * h, (im + sign * re) * h)
        return ((re + sign * im) * -h, (sign * re - im) * h)
    return (re * c - im * s, im * c + re * s)


def fft16(x, sign):
    inner = [fft4([x[4 * a + b] for a in range(4)], sign) for b in range(4)]
    out = [None] * 16
    for k in range(4):
        column = fft4([times(inner[b][k], b * k, sign) for b in range(4)], sign)
        for a in range(4):
            out[k + 4 * a] = column[a]
    return out


def atom_weights(w_ref, cells_ref, lo):
    at = slice(lo, lo + TILE)
    lx = cells_ref[0:1, at] & (BX - 1)
    ly = cells_ref[1:2, at] & (BY - 1)
    lx = jnp.broadcast_to(lx, (8, TILE))
    dy = lax.broadcasted_iota(jnp.int32, (8, TILE), 0) - ly
    on_y = [dy == j for j in range(4)]
    on_x = [lx == x for x in range(BX)]
    zero = jnp.zeros((8, TILE), F32)
    rows = [[None] * 4 for _ in range(4)]
    for i in range(4):
        for k in range(4):
            value = zero
            for j in range(4):
                row = jnp.broadcast_to(w_ref[16 * i + 4 * j + k : 16 * i + 4 * j + k + 1, at], (8, TILE))
                value = jnp.where(on_y[j], row, value)
            rows[i][k] = value
    spread = [[None] * 4 for _ in range(EX)]
    for x in range(EX):
        for k in range(4):
            value = zero
            for i in range(4):
                if 0 <= x - i < BX:
                    value = jnp.where(on_x[x - i], rows[i][k], value)
            spread[x][k] = value
    return spread


def z_hits(cells_ref, lo, k):
    bz = cells_ref[2:3, lo : lo + TILE]
    z = lax.broadcasted_iota(jnp.int32, (MESH, TILE), 0)
    return jnp.where(z == ((bz + k) & (MESH - 1)), 1.0, 0.0).astype(BF16)


def scatter_kernel(cot_in, w_in, cells_in, m_in, out_ref, cot_ref, w_ref, cells_ref, m_ref, hit_ref, den_ref, sems):
    pairs = ((cells_in, cells_ref), (cot_in, cot_ref), (w_in, w_ref), (m_in, m_ref))
    copies = [pltpu.make_async_copy(a, b, sems.at[i]) for i, (a, b) in enumerate(pairs)]
    for copy in copies:
        copy.start()
    for copy in copies[:3]:
        copy.wait()
    atoms = cot_ref.shape[1]
    for t in range(atoms // TILE):
        lo = t * TILE
        slot = t % 2
        spread = atom_weights(w_ref, cells_ref, lo)
        bz = jnp.broadcast_to(cells_ref[2:3, lo : lo + TILE], (TILE, TILE)).T
        zz = lax.broadcasted_iota(jnp.int32, (TILE, MESH), 1)
        for k in range(4):
            hit_ref[slot, k * TILE : (k + 1) * TILE, :] = jnp.where(zz == ((bz + k) & (MESH - 1)), 1.0, 0.0).astype(BF16)
        hit = hit_ref[slot]
        for c in range(0, CH, 2):
            cots = [jnp.broadcast_to(cot_ref[c + h : c + h + 1, lo : lo + TILE], (8, TILE)) for h in range(2)]
            hs, ls = [], []
            for k in range(4):
                g = jnp.concatenate([spread[x][k] * cots[h] for h in range(2) for x in range(EX)], axis=0)
                high, low = split(g)
                hs.append(high)
                ls.append(low)
            part = mm(jnp.concatenate(hs, axis=1), hit) + mm(jnp.concatenate(ls, axis=1), hit)
            at = slice(c * ROWS, (c + 2) * ROWS)
            if t == 0:
                den_ref[at, :] = part
            else:
                den_ref[at, :] += part
    copies[3].wait()
    mh, ml = m_ref[0], m_ref[1]
    for c in range(CH):
        rows = jnp.concatenate([den_ref[c * ROWS : (c + 1) * ROWS, :], jnp.zeros((LANES - ROWS, MESH), F32)], axis=0)
        high, low = split(rows)
        nt = ((1,), (1,))
        out_ref[c * 128 : (c + 1) * 128, :] = (
            mm(mh, high, nt) + mm(ml, high, nt) + mm(mh, low, nt)
        )


def plane_kernel(in_ref, filt_ref, fh_ref, fl_ref, tw_ref, sh_ref, sl_ref, third_ref, lh_ref, ll_ref, out_ref):
    rows = []
    for p8 in range(PY // 8):
        pair = jnp.concatenate([in_ref[512 * p8 : 512 * p8 + 256, :], in_ref[512 * p8 + 256 : 512 * p8 + 512, :]], axis=1)
        high, low = split(pair)
        part = mm(fh_ref[...], high) + mm(fl_ref[...], high) + mm(fh_ref[...], low)
        for half in (part[:, :LANES], part[:, LANES:]):
            for p in range(4):
                rows.append((half[64 * p : 64 * p + 32], half[64 * p + 32 : 64 * p + 64]))
    rows = fft16(rows, -1)
    turned = []
    for k in range(PY):
        at = slice(PZ * k, PZ * (k + 1))
        tr, ti = tw_ref[0, at, :], tw_ref[1, at, :]
        re, im = rows[k]
        turned.append(jnp.concatenate([re * tr - im * ti, im * tr + re * ti], axis=1))
    back = []
    step = 8
    for g in range(0, PY, step):
        at = slice(PZ * g, PZ * (g + step))
        high, low = split(jnp.concatenate(turned[g : g + step], axis=0))
        spec = mm(high, sh_ref[...]) + mm(high, sl_ref[...]) + mm(low, sh_ref[...])
        sides = []
        for ab in range(2):
            high, low = split(spec[:, 128 * ab : 128 * ab + 128] * filt_ref[at, 128 * ab : 128 * ab + 128])
            sides.append(mm(jnp.concatenate([high, low], axis=1), third_ref[...]))
        for k in range(step):
            here = slice(PZ * k, PZ * (k + 1))
            tr, ti = tw_ref[0, PZ * (g + k) : PZ * (g + k + 1), :], tw_ref[1, PZ * (g + k) : PZ * (g + k + 1), :]
            cols = []
            for side in sides:
                re, im = side[here, :LANES], side[here, LANES:]
                cols.append((re * tr + im * ti, im * tr - re * ti))
            back.append(cols)
    a = fft16([cols[0] for cols in back], 1)
    b = fft16([cols[1] for cols in back], 1)
    for p in range(0, PY, 4):
        stack = []
        for o in (p, p + 2):
            stack.append(jnp.concatenate([a[o][0], a[o][1], b[o][0], b[o][1], a[o + 1][0], a[o + 1][1], b[o + 1][0], b[o + 1][1]], axis=0))
        high, low = split(jnp.concatenate(stack, axis=1))
        part = mm(lh_ref[...], high) + mm(ll_ref[...], high) + mm(lh_ref[...], low)
        out_ref[64 * p : 64 * (p + 2), :] = part[:, :LANES]
        out_ref[64 * (p + 2) : 64 * (p + 4), :] = part[:, LANES:]


def gather_kernel(in_ref, w_ref, cells_ref, b_ref, out_ref, pot_ref, hit_ref):
    atoms = out_ref.shape[1]
    for c in range(0, CH, 2):
        pots = []
        for h in range(2):
            high, low = split(in_ref[(c + h) * 128 : (c + h + 1) * 128, :].T)
            pot = mm(jnp.concatenate([high, low], axis=1), b_ref[...])
            pots.append(pot[:ROWS, :MESH] + pot[:ROWS, MESH:])
        high, low = split(jnp.concatenate(pots, axis=0))
        pot_ref[c * ROWS : (c + 2) * ROWS, 0:MESH] = high
        pot_ref[c * ROWS : (c + 2) * ROWS, MESH : 2 * MESH] = low
    for t in range(atoms // TILE):
        lo = t * TILE
        slot = t % 2
        spread = atom_weights(w_ref, cells_ref, lo)
        for k in range(4):
            hit = z_hits(cells_ref, lo, k)
            hit_ref[slot, 0:MESH, k * TILE : (k + 1) * TILE] = hit
            hit_ref[slot, MESH : 2 * MESH, k * TILE : (k + 1) * TILE] = hit
        for c in range(0, CH, 2):
            near = mm(pot_ref[c * ROWS : (c + 2) * ROWS, :], hit_ref[slot])
            for h in range(2):
                sums = [None] * 4
                for x in range(EX):
                    for k in range(4):
                        r = h * ROWS + 8 * x
                        term = spread[x][k] * near[r : r + 8, k * TILE : (k + 1) * TILE]
                        sums[k] = term if x == 0 else sums[k] + term
                total = (sums[0] + sums[1]) + (sums[2] + sums[3])
                out_ref[c + h : c + h + 1, lo : lo + TILE] = jnp.sum(total, axis=0, keepdims=True)


def call(kernel, out_shape, scratch, flops, moved, *args, space=pltpu.VMEM, limit=40):
    return pl.pallas_call(
        kernel,
        out_shape=jax.ShapeDtypeStruct(out_shape, F32),
        in_specs=[pl.BlockSpec(memory_space=space)] * len(args),
        out_specs=pl.BlockSpec(memory_space=pltpu.VMEM),
        scratch_shapes=scratch,
        compiler_params=pltpu.CompilerParams(vmem_limit_bytes=limit * 1024 * 1024),
        cost_estimate=pl.CostEstimate(flops=flops, bytes_accessed=moved, transcendentals=0),
    )(*args)


def scatter(cotangent, spline_weights, base_cells):
    forth, _ = z_tables()
    table = np.stack(halves(forth))
    args = (cotangent, spline_weights, base_cells, table)
    scratch = [pltpu.VMEM(a.shape, a.dtype) for a in args] + [
        pltpu.VMEM((2, 4 * TILE, MESH), BF16),
        pltpu.VMEM((CH * ROWS, MESH), F32),
        pltpu.SemaphoreType.DMA((4,)),
    ]
    return call(scatter_kernel, (CH * 128, LANES), scratch, 3 * 10**9, 10**6, *args, space=pltpu.HBM, limit=60)


def plane(blocks, filt):
    first, twist, second, third, last = plane_tables()
    return call(
        plane_kernel, (PY * PZ * 2, LANES), [], 10**9, 2 * 10**6,
        blocks, filt, *halves(first), twist, *halves(second), third, *halves(last),
    )


def gather(blocks, spline_weights, base_cells):
    _, back = z_tables()
    atoms = spline_weights.shape[1]
    high, low = halves(back)
    table = np.block([[high, low], [high, low]])
    scratch = [
        pltpu.VMEM((CH * ROWS, 2 * MESH), BF16),
        pltpu.VMEM((2, 2 * MESH, 4 * TILE), BF16),
    ]
    return call(gather_kernel, (CH, atoms), scratch, 3 * 10**9, 10**6, blocks, spline_weights, base_cells, table)


def plane_filter(spectral_filter):
    p, q = lax.axis_index("py"), lax.axis_index("pz")
    half = PZ // 2
    pair = lax.all_to_all(spectral_filter.reshape(PY, 2, BX, MESH), "py", 0, 0)
    even = lax.ppermute(pair[:, 0], "pz", [(0, half)])
    mine = jnp.where(q < half, pair[:, 1], pair[:, 0])
    shared = (q == half) & (p % 2 == 0)
    both = jnp.stack([jnp.where(shared, even, mine), mine], axis=1)
    both = both.reshape(4, 4, 2, 8, 8, 16).transpose(5, 1, 3, 2, 4, 0).reshape(PY * PZ, 2, 1, 32)
    return jnp.broadcast_to(both, (PY * PZ, 2, 4, 32)).reshape(PY * PZ, 256)


def exchange(blocks):
    return lax.all_to_all(blocks.reshape(PY * PZ, 2, LANES), ("py", "pz"), 0, 0).reshape(PY * PZ * 2, LANES)


def on_device(cotangent, spline_weights, base_cells, spectral_filter):
    filt = plane_filter(spectral_filter)
    blocks = scatter(cotangent, spline_weights, base_cells)
    blocks = exchange(blocks)
    blocks = plane(blocks, filt)
    blocks = exchange(blocks)
    return gather(blocks, spline_weights, base_cells)


def solution(mesh):
    return jax.shard_map(
        on_device,
        mesh=mesh,
        in_specs=(
            P(None, ("py", "pz")),
            P(None, ("py", "pz")),
            P(None, ("py", "pz")),
            P(None, "pz", "py", None),
        ),
        out_specs=P(None, ("py", "pz")),
        check_vma=False,
    )
```

```python
import math

import jax
import jax.numpy as jnp
import ml_dtypes
import numpy as np
from jax import lax
from jax.experimental import pallas as pl
from jax.experimental.pallas import tpu as pltpu
from jax.sharding import PartitionSpec as P

MESH = 128
CH = 8
PY = 16
PZ = 32
BX = MESH // PY
BY = MESH // PZ
EX = BX + 3
ROWS = EX * 8
LANES = 128
TILE = 128

F32 = jnp.float32
BF16 = jnp.bfloat16


def halves(table):
    high = table.astype(ml_dtypes.bfloat16)
    low = (table - high.astype(np.float64)).astype(ml_dtypes.bfloat16)
    return high, low


def turn(numerator, denominator):
    angle = 2.0 * math.pi * (numerator % denominator) / denominator
    return np.cos(angle) + 1j * np.sin(angle)


def z_tables():
    z = np.arange(MESH)
    forth = np.zeros((2, PZ, 2, MESH))
    back = np.zeros((2, PZ, 2, MESH))
    scale = 1.0 / float(MESH) ** 3
    for s in range(2):
        for q in range(PZ):
            kz = 4 * q + 2 * s + (1 if q < PZ // 2 else 0)
            wave = turn(kz * z, MESH)
            forth[s, q, 0] = wave.real
            forth[s, q, 1] = -wave.imag
            back[s, q, 0] = 2.0 * scale * wave.real
            back[s, q, 1] = -2.0 * scale * wave.imag
    sign = 1.0 - 2.0 * (z % 2)
    forth[0, PZ // 2, 0] = 1.0
    forth[0, PZ // 2, 1] = sign
    back[0, PZ // 2, 0] = scale
    back[0, PZ // 2, 1] = scale * sign
    return forth.reshape(128, MESH), back.reshape(128, MESH)


def plane_tables():
    k0 = np.arange(PZ)
    wave = turn(-np.outer(k0, np.arange(PZ)), PZ)
    first = np.zeros((2, PZ, PZ, 2))
    first[0, :, :, 0] = wave.real
    first[0, :, :, 1] = -wave.imag
    first[1, :, :, 0] = wave.imag
    first[1, :, :, 1] = wave.real
    first = np.kron(np.eye(4), first.reshape(64, 64))
    xl = np.zeros(LANES, np.int64)
    yl = np.zeros(LANES, np.int64)
    used = np.zeros(LANES)
    for x in range(EX):
        for y in range(BY + 3):
            xl[8 * x + y] = x
            yl[8 * x + y] = y
            used[8 * x + y] = 1.0
    kx0 = np.repeat(np.arange(PY), PZ)
    ky0 = np.tile(np.arange(PZ), PY)
    twist = turn(-(kx0[:, None] * xl[None] + ky0[:, None] * yl[None]), MESH) * used
    m = np.repeat(np.arange(8), 4)
    n = np.tile(np.arange(4), 8)
    fine = turn(-(4 * m[None] * xl[:, None] + 8 * n[None] * yl[:, None]), 32) * used[:, None]
    second = np.zeros((2, LANES, 4, 2, 32))
    second[0, :, :, 0] = fine.real[:, None]
    second[1, :, :, 0] = -fine.imag[:, None]
    second[0, :, :, 1] = fine.imag[:, None]
    second[1, :, :, 1] = fine.real[:, None]
    third = np.zeros((2, 32, 2, LANES))
    third[0, :, 0] = fine.real.T
    third[1, :, 0] = fine.imag.T
    third[0, :, 1] = -fine.imag.T
    third[1, :, 1] = fine.real.T
    high, low = halves(third.reshape(64, 256))
    third = np.concatenate([high, low, high, low])
    last = np.zeros((PZ, 2, 2, 2, PZ))
    last[:, 0, 0, 0] = wave.real.T
    last[:, 0, 0, 1] = wave.imag.T
    last[:, 1, 1, 0] = -wave.imag.T
    last[:, 1, 1, 1] = wave.real.T
    last = np.kron(np.eye(2), last.reshape(64, 128))
    twist = np.stack([twist.real, twist.imag]).astype(np.float32)
    return first, twist, second.reshape(256, 256), third, last


def split(value):
    high = value.astype(BF16)
    return high, (value - high.astype(F32)).astype(BF16)


def mm(a, b, dims=((1,), (0,))):
    return lax.dot_general(a, b, (dims, ((), ())), preferred_element_type=F32)


def fft4(x, sign):
    (ar, ai), (br, bi), (cr, ci), (dr, di) = x
    sr, si, tr, ti = ar + cr, ai + ci, ar - cr, ai - ci
    ur, ui, vr, vi = br + dr, bi + di, br - dr, bi - di
    if sign < 0:
        return [(sr + ur, si + ui), (tr + vi, ti - vr), (sr - ur, si - ui), (tr - vi, ti + vr)]
    return [(sr + ur, si + ui), (tr - vi, ti + vr), (sr - ur, si - ui), (tr + vi, ti - vr)]


def times(value, k, sign):
    re, im = value
    k %= 16
    if k == 0:
        return value
    if k == 4:
        return (-sign * im, sign * re)
    c, s = math.cos(2.0 * math.pi * k / 16), sign * math.sin(2.0 * math.pi * k / 16)
    if k in (2, 6):
        h = math.sqrt(0.5)
        if k == 2:
            return ((re - sign * im) * h, (im + sign * re) * h)
        return ((re + sign * im) * -h, (sign * re - im) * h)
    return (re * c - im * s, im * c + re * s)


def fft16(x, sign):
    inner = [fft4([x[4 * a + b] for a in range(4)], sign) for b in range(4)]
    out = [None] * 16
    for k in range(4):
        column = fft4([times(inner[b][k], b * k, sign) for b in range(4)], sign)
        for a in range(4):
            out[k + 4 * a] = column[a]
    return out


def atom_weights(w_ref, cells_ref, lo):
    at = slice(lo, lo + TILE)
    lx = cells_ref[0:1, at] & (BX - 1)
    ly = cells_ref[1:2, at] & (BY - 1)
    lx = jnp.broadcast_to(lx, (8, TILE))
    dy = lax.broadcasted_iota(jnp.int32, (8, TILE), 0) - ly
    on_y = [dy == j for j in range(4)]
    on_x = [lx == x for x in range(BX)]
    zero = jnp.zeros((8, TILE), F32)
    rows = [[None] * 4 for _ in range(4)]
    for i in range(4):
        for k in range(4):
            value = zero
            for j in range(4):
                row = jnp.broadcast_to(w_ref[16 * i + 4 * j + k : 16 * i + 4 * j + k + 1, at], (8, TILE))
                value = jnp.where(on_y[j], row, value)
            rows[i][k] = value
    spread = [[None] * 4 for _ in range(EX)]
    for x in range(EX):
        for k in range(4):
            value = zero
            for i in range(4):
                if 0 <= x - i < BX:
                    value = jnp.where(on_x[x - i], rows[i][k], value)
            spread[x][k] = value
    return spread


def z_hits(cells_ref, lo, k):
    bz = cells_ref[2:3, lo : lo + TILE]
    z = lax.broadcasted_iota(jnp.int32, (MESH, TILE), 0)
    return jnp.where(z == ((bz + k) & (MESH - 1)), 1.0, 0.0).astype(BF16)


def scatter_kernel(cot_in, w_in, cells_in, m_in, out_ref, cot_ref, w_ref, cells_ref, m_ref, hit_ref, den_ref, sems):
    pairs = ((cells_in, cells_ref), (cot_in, cot_ref), (w_in, w_ref), (m_in, m_ref))
    copies = [pltpu.make_async_copy(a, b, sems.at[i]) for i, (a, b) in enumerate(pairs)]
    for copy in copies:
        copy.start()
    for copy in copies[:3]:
        copy.wait()
    atoms = cot_ref.shape[1]
    for t in range(atoms // TILE):
        lo = t * TILE
        slot = t % 2
        spread = atom_weights(w_ref, cells_ref, lo)
        bz = jnp.broadcast_to(cells_ref[2:3, lo : lo + TILE], (TILE, TILE)).T
        zz = lax.broadcasted_iota(jnp.int32, (TILE, MESH), 1)
        for k in range(4):
            hit_ref[slot, k * TILE : (k + 1) * TILE, :] = jnp.where(zz == ((bz + k) & (MESH - 1)), 1.0, 0.0).astype(BF16)
        hit = hit_ref[slot]
        group = 4
        for c in range(0, CH, group):
            cots = [jnp.broadcast_to(cot_ref[c + h : c + h + 1, lo : lo + TILE], (8, TILE)) for h in range(group)]
            hs, ls = [], []
            for k in range(4):
                g = jnp.concatenate([spread[x][k] * cots[h] for h in range(group) for x in range(EX)], axis=0)
                high, low = split(g)
                hs.append(high)
                ls.append(low)
            both = jnp.concatenate([jnp.concatenate(hs, axis=1), jnp.concatenate(ls, axis=1)], axis=0)
            part = mm(both, hit)
            part = part[: group * ROWS] + part[group * ROWS :]
            at = slice(c * ROWS, (c + group) * ROWS)
            if t == 0:
                den_ref[at, :] = part
            else:
                den_ref[at, :] += part
    copies[3].wait()
    mh, ml = m_ref[0], m_ref[1]
    for c in range(CH):
        rows = jnp.concatenate([den_ref[c * ROWS : (c + 1) * ROWS, :], jnp.zeros((LANES - ROWS, MESH), F32)], axis=0)
        high, low = split(rows)
        nt = ((1,), (1,))
        out_ref[c * 128 : (c + 1) * 128, :] = (
            mm(mh, high, nt) + mm(ml, high, nt) + mm(mh, low, nt)
        )


def plane_kernel(in_ref, filt_ref, fh_ref, fl_ref, tw_ref, sh_ref, sl_ref, third_ref, lh_ref, ll_ref, out_ref):
    rows = []
    for p8 in range(PY // 8):
        pair = jnp.concatenate([in_ref[512 * p8 : 512 * p8 + 256, :], in_ref[512 * p8 + 256 : 512 * p8 + 512, :]], axis=1)
        high, low = split(pair)
        part = mm(fh_ref[...], high) + mm(fl_ref[...], high) + mm(fh_ref[...], low)
        for half in (part[:, :LANES], part[:, LANES:]):
            for p in range(4):
                rows.append((half[64 * p : 64 * p + 32], half[64 * p + 32 : 64 * p + 64]))
    rows = fft16(rows, -1)
    turned = []
    for k in range(PY):
        at = slice(PZ * k, PZ * (k + 1))
        tr, ti = tw_ref[0, at, :], tw_ref[1, at, :]
        re, im = rows[k]
        turned.append(jnp.concatenate([re * tr - im * ti, im * tr + re * ti], axis=1))
    back = []
    step = 8
    for g in range(0, PY, step):
        at = slice(PZ * g, PZ * (g + step))
        high, low = split(jnp.concatenate(turned[g : g + step], axis=0))
        spec = mm(high, sh_ref[...]) + mm(high, sl_ref[...]) + mm(low, sh_ref[...])
        sides = []
        for ab in range(2):
            high, low = split(spec[:, 128 * ab : 128 * ab + 128] * filt_ref[at, 128 * ab : 128 * ab + 128])
            sides.append(mm(jnp.concatenate([high, low], axis=1), third_ref[...]))
        for k in range(step):
            here = slice(PZ * k, PZ * (k + 1))
            tr, ti = tw_ref[0, PZ * (g + k) : PZ * (g + k + 1), :], tw_ref[1, PZ * (g + k) : PZ * (g + k + 1), :]
            cols = []
            for side in sides:
                re, im = side[here, :LANES], side[here, LANES:]
                cols.append((re * tr + im * ti, im * tr - re * ti))
            back.append(cols)
    a = fft16([cols[0] for cols in back], 1)
    b = fft16([cols[1] for cols in back], 1)
    for p in range(0, PY, 4):
        stack = []
        for o in (p, p + 2):
            stack.append(jnp.concatenate([a[o][0], a[o][1], b[o][0], b[o][1], a[o + 1][0], a[o + 1][1], b[o + 1][0], b[o + 1][1]], axis=0))
        high, low = split(jnp.concatenate(stack, axis=1))
        part = mm(lh_ref[...], high) + mm(ll_ref[...], high) + mm(lh_ref[...], low)
        out_ref[64 * p : 64 * (p + 2), :] = part[:, :LANES]
        out_ref[64 * (p + 2) : 64 * (p + 4), :] = part[:, LANES:]


def gather_kernel(in_ref, w_ref, cells_ref, b_ref, out_ref, pot_ref, hit_ref):
    atoms = out_ref.shape[1]
    for c in range(0, CH, 2):
        pots = []
        for h in range(2):
            high, low = split(in_ref[(c + h) * 128 : (c + h + 1) * 128, :].T)
            pot = mm(jnp.concatenate([high, low], axis=1), b_ref[...])
            pots.append(pot[:ROWS, :MESH] + pot[:ROWS, MESH:])
        high, low = split(jnp.concatenate(pots, axis=0))
        pot_ref[c * ROWS : (c + 2) * ROWS, 0:MESH] = high
        pot_ref[c * ROWS : (c + 2) * ROWS, MESH : 2 * MESH] = low
    for t in range(atoms // TILE):
        lo = t * TILE
        slot = t % 2
        spread = atom_weights(w_ref, cells_ref, lo)
        for k in range(4):
            hit = z_hits(cells_ref, lo, k)
            hit_ref[slot, 0:MESH, k * TILE : (k + 1) * TILE] = hit
            hit_ref[slot, MESH : 2 * MESH, k * TILE : (k + 1) * TILE] = hit
        for c in range(0, CH, 4):
            near = mm(pot_ref[c * ROWS : (c + 4) * ROWS, :], hit_ref[slot])
            for h in range(4):
                sums = [None] * 4
                for x in range(EX):
                    for k in range(4):
                        r = h * ROWS + 8 * x
                        term = spread[x][k] * near[r : r + 8, k * TILE : (k + 1) * TILE]
                        sums[k] = term if x == 0 else sums[k] + term
                total = (sums[0] + sums[1]) + (sums[2] + sums[3])
                out_ref[c + h : c + h + 1, lo : lo + TILE] = jnp.sum(total, axis=0, keepdims=True)


def call(kernel, out_shape, scratch, flops, moved, *args, space=pltpu.VMEM, limit=40):
    return pl.pallas_call(
        kernel,
        out_shape=jax.ShapeDtypeStruct(out_shape, F32),
        in_specs=[pl.BlockSpec(memory_space=space)] * len(args),
        out_specs=pl.BlockSpec(memory_space=pltpu.VMEM),
        scratch_shapes=scratch,
        compiler_params=pltpu.CompilerParams(vmem_limit_bytes=limit * 1024 * 1024),
        cost_estimate=pl.CostEstimate(flops=flops, bytes_accessed=moved, transcendentals=0),
    )(*args)


def scatter(cotangent, spline_weights, base_cells):
    forth, _ = z_tables()
    table = np.stack(halves(forth))
    args = (cotangent, spline_weights, base_cells, table)
    scratch = [pltpu.VMEM(a.shape, a.dtype) for a in args] + [
        pltpu.VMEM((2, 4 * TILE, MESH), BF16),
        pltpu.VMEM((CH * ROWS, MESH), F32),
        pltpu.SemaphoreType.DMA((4,)),
    ]
    return call(scatter_kernel, (CH * 128, LANES), scratch, 3 * 10**9, 10**6, *args, space=pltpu.HBM, limit=60)


def plane(blocks, filt):
    first, twist, second, third, last = plane_tables()
    return call(
        plane_kernel, (PY * PZ * 2, LANES), [], 10**9, 2 * 10**6,
        blocks, filt, *halves(first), twist, *halves(second), third, *halves(last),
    )


def gather(blocks, spline_weights, base_cells):
    _, back = z_tables()
    atoms = spline_weights.shape[1]
    high, low = halves(back)
    table = np.block([[high, low], [high, low]])
    scratch = [
        pltpu.VMEM((CH * ROWS, 2 * MESH), BF16),
        pltpu.VMEM((2, 2 * MESH, 4 * TILE), BF16),
    ]
    return call(gather_kernel, (CH, atoms), scratch, 3 * 10**9, 10**6, blocks, spline_weights, base_cells, table)


def filter_kernel(flag_ref, pair_ref, even_ref, pick_ref, out_ref):
    mine, other = [], []
    for p in range(PY):
        row = jnp.where(flag_ref[0] > 0, pair_ref[p, 1], pair_ref[p, 0])
        mine.append(row)
        other.append(jnp.where(flag_ref[1] > 0, even_ref[p], row))
    lane = lax.broadcasted_iota(jnp.int32, (PZ, LANES), 1) & 3
    for ab, rows in enumerate((other, mine)):
        rest = jnp.concatenate(rows, axis=0)
        parts = []
        for _ in range(3):
            part = rest.astype(BF16)
            rest = rest - part.astype(F32)
            parts.append(part)
        wide = mm(jnp.concatenate(parts, axis=0), pick_ref[...])
        wide = (wide[:MESH] + wide[MESH : 2 * MESH]) + wide[2 * MESH :]
        for k in range(PY):
            at = slice(LANES * k, LANES * (k + 1))
            value = wide[0:PZ, at]
            for n in range(1, 4):
                value = jnp.where(lane == n, wide[PZ * n : PZ * (n + 1), at], value)
            out_ref[PZ * k : PZ * (k + 1), LANES * ab : LANES * (ab + 1)] = value


def plane_filter(spectral_filter):
    p, q = lax.axis_index("py"), lax.axis_index("pz")
    half = PZ // 2
    pair = lax.all_to_all(spectral_filter.reshape(PY, 2, BX, MESH), "py", 0, 0)
    even = lax.ppermute(pair[:, 0], "pz", [(0, half)])
    flags = jnp.stack([q < half, (q == half) & (p % 2 == 0)]).astype(jnp.int32)
    pick = np.zeros((8, PY, PY, 4, 8, 4))
    for m in range(8):
        for k in range(PY):
            pick[m, k, k, :, m, :] = 1.0
    pick = pick.reshape(MESH, PY * LANES).astype(ml_dtypes.bfloat16)
    vmem = pl.BlockSpec(memory_space=pltpu.VMEM)
    return pl.pallas_call(
        filter_kernel,
        out_shape=jax.ShapeDtypeStruct((PY * PZ, 2 * LANES), F32),
        in_specs=[pl.BlockSpec(memory_space=pltpu.SMEM), vmem, vmem, vmem],
        out_specs=vmem,
        compiler_params=pltpu.CompilerParams(vmem_limit_bytes=32 * 1024 * 1024),
        cost_estimate=pl.CostEstimate(flops=10**9, bytes_accessed=10**6, transcendentals=0),
    )(flags, pair, even, pick)


def exchange(blocks):
    return lax.all_to_all(blocks.reshape(PY * PZ, 2, LANES), ("py", "pz"), 0, 0).reshape(PY * PZ * 2, LANES)


def on_device(cotangent, spline_weights, base_cells, spectral_filter):
    filt = plane_filter(spectral_filter)
    blocks = scatter(cotangent, spline_weights, base_cells)
    blocks = exchange(blocks)
    blocks = plane(blocks, filt)
    blocks = exchange(blocks)
    return gather(blocks, spline_weights, base_cells)


def solution(mesh):
    return jax.shard_map(
        on_device,
        mesh=mesh,
        in_specs=(
            P(None, ("py", "pz")),
            P(None, ("py", "pz")),
            P(None, ("py", "pz")),
            P(None, "pz", "py", None),
        ),
        out_specs=P(None, ("py", "pz")),
        check_vma=False,
    )
```

```python
import math

import jax
import jax.numpy as jnp
import ml_dtypes
import numpy as np
from jax import lax
from jax.experimental import pallas as pl
from jax.experimental.pallas import tpu as pltpu
from jax.sharding import PartitionSpec as P

MESH = 128
CH = 8
PY = 16
PZ = 32
BX = MESH // PY
BY = MESH // PZ
EX = BX + 3
ROWS = EX * 8
LANES = 128
OWN = BX * 8
EDGE = 3 * 8
TILE = 128

F32 = jnp.float32
BF16 = jnp.bfloat16


def halves(table):
    high = table.astype(ml_dtypes.bfloat16)
    low = (table - high.astype(np.float64)).astype(ml_dtypes.bfloat16)
    return high, low


def turn(numerator, denominator):
    angle = 2.0 * math.pi * (numerator % denominator) / denominator
    return np.cos(angle) + 1j * np.sin(angle)


def z_tables():
    z = np.arange(MESH)
    forth = np.zeros((2, PZ, 2, MESH))
    back = np.zeros((2, PZ, 2, MESH))
    scale = 1.0 / float(MESH) ** 3
    for s in range(2):
        for q in range(PZ):
            kz = 4 * q + 2 * s + (1 if q < PZ // 2 else 0)
            wave = turn(kz * z, MESH)
            forth[s, q, 0] = wave.real
            forth[s, q, 1] = -wave.imag
            back[s, q, 0] = 2.0 * scale * wave.real
            back[s, q, 1] = -2.0 * scale * wave.imag
    sign = 1.0 - 2.0 * (z % 2)
    forth[0, PZ // 2, 0] = 1.0
    forth[0, PZ // 2, 1] = sign
    back[0, PZ // 2, 0] = scale
    back[0, PZ // 2, 1] = scale * sign
    return forth.reshape(128, MESH), back.reshape(64, 2 * MESH)


def plane_tables():
    k0 = np.arange(PZ)
    wave = turn(-np.outer(k0, np.arange(PZ)), PZ)
    first = np.zeros((2, PZ, PZ, 2))
    first[0, :, :, 0] = wave.real
    first[0, :, :, 1] = -wave.imag
    first[1, :, :, 0] = wave.imag
    first[1, :, :, 1] = wave.real
    first = np.kron(np.eye(4), first.reshape(64, 64))
    xl = np.zeros(LANES, np.int64)
    yl = np.zeros(LANES, np.int64)
    used = np.zeros(LANES)
    for x in range(EX):
        for y in range(BY + 3):
            xl[8 * x + y] = x
            yl[8 * x + y] = y
            used[8 * x + y] = 1.0
    kx0 = np.repeat(np.arange(PY), PZ)
    ky0 = np.tile(np.arange(PZ), PY)
    twist = turn(-(kx0[:, None] * xl[None] + ky0[:, None] * yl[None]), MESH) * used
    m = np.repeat(np.arange(8), 4)
    n = np.tile(np.arange(4), 8)
    fine = turn(-(4 * m[None] * xl[:, None] + 8 * n[None] * yl[:, None]), 32) * used[:, None]
    second = np.zeros((2, LANES, 4, 2, 32))
    second[0, :, :, 0] = fine.real[:, None]
    second[1, :, :, 0] = -fine.imag[:, None]
    second[0, :, :, 1] = fine.imag[:, None]
    second[1, :, :, 1] = fine.real[:, None]
    fine = np.where(np.arange(LANES)[:, None] < OWN, fine, 0.0)
    third = np.zeros((2, 32, 2, LANES))
    third[0, :, 0] = fine.real.T
    third[1, :, 0] = fine.imag.T
    third[0, :, 1] = -fine.imag.T
    third[1, :, 1] = fine.real.T
    high, low = halves(third.reshape(64, 256))
    third = np.concatenate([high, low, high, low])
    last = np.zeros((2, PZ, 2, 2, PZ))
    last[0, :, 0, 0] = wave.real.T
    last[0, :, 0, 1] = wave.imag.T
    last[1, :, 1, 0] = -wave.imag.T
    last[1, :, 1, 1] = wave.real.T
    last = np.kron(np.eye(2), last.reshape(64, 128))
    twist = np.stack([twist.real, twist.imag]).astype(np.float32)
    return first, twist, second.reshape(256, 256), third, last


def split(value):
    high = value.astype(BF16)
    return high, (value - high.astype(F32)).astype(BF16)


def mm(a, b, dims=((1,), (0,))):
    return lax.dot_general(a, b, (dims, ((), ())), preferred_element_type=F32)


def fft4(x, sign):
    (ar, ai), (br, bi), (cr, ci), (dr, di) = x
    sr, si, tr, ti = ar + cr, ai + ci, ar - cr, ai - ci
    ur, ui, vr, vi = br + dr, bi + di, br - dr, bi - di
    if sign < 0:
        return [(sr + ur, si + ui), (tr + vi, ti - vr), (sr - ur, si - ui), (tr - vi, ti + vr)]
    return [(sr + ur, si + ui), (tr - vi, ti + vr), (sr - ur, si - ui), (tr + vi, ti - vr)]


def times(value, k, sign):
    re, im = value
    k %= 16
    if k == 0:
        return value
    if k == 4:
        return (-sign * im, sign * re)
    c, s = math.cos(2.0 * math.pi * k / 16), sign * math.sin(2.0 * math.pi * k / 16)
    if k in (2, 6):
        h = math.sqrt(0.5)
        if k == 2:
            return ((re - sign * im) * h, (im + sign * re) * h)
        return ((re + sign * im) * -h, (sign * re - im) * h)
    return (re * c - im * s, im * c + re * s)


def fft16(x, sign):
    inner = [fft4([x[4 * a + b] for a in range(4)], sign) for b in range(4)]
    out = [None] * 16
    for k in range(4):
        column = fft4([times(inner[b][k], b * k, sign) for b in range(4)], sign)
        for a in range(4):
            out[k + 4 * a] = column[a]
    return out


def atom_weights(w_ref, cells_ref, lo, layers):
    at = slice(lo, lo + TILE)
    lx = cells_ref[0:1, at] & (BX - 1)
    ly = cells_ref[1:2, at] & (BY - 1)
    lx = jnp.broadcast_to(lx, (8, TILE))
    dy = lax.broadcasted_iota(jnp.int32, (8, TILE), 0) - ly
    on_y = [dy == j for j in range(4)]
    on_x = [lx == x for x in range(BX)]
    zero = jnp.zeros((8, TILE), F32)
    rows = [[None] * 4 for _ in range(4)]
    for i in range(4):
        for k in range(4):
            value = zero
            for j in range(4):
                row = jnp.broadcast_to(w_ref[16 * i + 4 * j + k : 16 * i + 4 * j + k + 1, at], (8, TILE))
                value = jnp.where(on_y[j], row, value)
            rows[i][k] = value
    spread = []
    for x in layers:
        values = []
        for k in range(4):
            value = zero
            for i in range(4):
                if 0 <= x - i < BX:
                    value = jnp.where(on_x[x - i], rows[i][k], value)
            values.append(value)
        spread.append(values)
    return spread


def z_hits(cells_ref, lo, k):
    bz = cells_ref[2:3, lo : lo + TILE]
    z = lax.broadcasted_iota(jnp.int32, (MESH, TILE), 0)
    return jnp.where(z == ((bz + k) & (MESH - 1)), 1.0, 0.0).astype(BF16)


def scatter_kernel(cot_in, w_in, cells_in, m_in, out_ref, cot_ref, w_ref, cells_ref, m_ref, hit_ref, den_ref, sems):
    pairs = ((cells_in, cells_ref), (cot_in, cot_ref), (w_in, w_ref), (m_in, m_ref))
    copies = [pltpu.make_async_copy(a, b, sems.at[i]) for i, (a, b) in enumerate(pairs)]
    for copy in copies:
        copy.start()
    for copy in copies[:3]:
        copy.wait()
    atoms = cot_ref.shape[1]
    for t in range(atoms // TILE):
        lo = t * TILE
        slot = t % 2
        spread = atom_weights(w_ref, cells_ref, lo, range(EX))
        bz = jnp.broadcast_to(cells_ref[2:3, lo : lo + TILE], (TILE, TILE)).T
        zz = lax.broadcasted_iota(jnp.int32, (TILE, MESH), 1)
        for k in range(4):
            hit_ref[slot, k * TILE : (k + 1) * TILE, :] = jnp.where(zz == ((bz + k) & (MESH - 1)), 1.0, 0.0).astype(BF16)
        hit = hit_ref[slot]
        group = 4
        for c in range(0, CH, group):
            cots = [jnp.broadcast_to(cot_ref[c + h : c + h + 1, lo : lo + TILE], (8, TILE)) for h in range(group)]
            hs, ls = [], []
            for k in range(4):
                g = jnp.concatenate([spread[x][k] * cots[h] for h in range(group) for x in range(EX)], axis=0)
                high, low = split(g)
                hs.append(high)
                ls.append(low)
            both = jnp.concatenate([jnp.concatenate(hs, axis=1), jnp.concatenate(ls, axis=1)], axis=0)
            part = mm(both, hit)
            part = part[: group * ROWS] + part[group * ROWS :]
            at = slice(c * ROWS, (c + group) * ROWS)
            if t == 0:
                den_ref[at, :] = part
            else:
                den_ref[at, :] += part
    copies[3].wait()
    mh, ml = m_ref[0], m_ref[1]
    for c in range(CH):
        rows = jnp.concatenate([den_ref[c * ROWS : (c + 1) * ROWS, :], jnp.zeros((LANES - ROWS, MESH), F32)], axis=0)
        high, low = split(rows)
        nt = ((1,), (1,))
        out_ref[c * 128 : (c + 1) * 128, :] = (
            mm(mh, high, nt) + mm(ml, high, nt) + mm(mh, low, nt)
        )


def plane_kernel(in_ref, filt_ref, fh_ref, fl_ref, tw_ref, sh_ref, sl_ref, third_ref, lh_ref, ll_ref, out_ref):
    rows = []
    for p8 in range(PY // 8):
        pair = jnp.concatenate([in_ref[512 * p8 : 512 * p8 + 256, :], in_ref[512 * p8 + 256 : 512 * p8 + 512, :]], axis=1)
        high, low = split(pair)
        part = mm(fh_ref[...], high) + mm(fl_ref[...], high) + mm(fh_ref[...], low)
        for half in (part[:, :LANES], part[:, LANES:]):
            for p in range(4):
                rows.append((half[64 * p : 64 * p + 32], half[64 * p + 32 : 64 * p + 64]))
    rows = fft16(rows, -1)
    turned = []
    for k in range(PY):
        at = slice(PZ * k, PZ * (k + 1))
        tr, ti = tw_ref[0, at, :], tw_ref[1, at, :]
        re, im = rows[k]
        turned.append(jnp.concatenate([re * tr - im * ti, im * tr + re * ti], axis=1))
    back = []
    step = 8
    for g in range(0, PY, step):
        at = slice(PZ * g, PZ * (g + step))
        high, low = split(jnp.concatenate(turned[g : g + step], axis=0))
        spec = mm(high, sh_ref[...]) + mm(high, sl_ref[...]) + mm(low, sh_ref[...])
        sides = []
        for ab in range(2):
            high, low = split(spec[:, 128 * ab : 128 * ab + 128] * filt_ref[at, 128 * ab : 128 * ab + 128])
            sides.append(mm(jnp.concatenate([high, low], axis=1), third_ref[...]))
        for k in range(step):
            here = slice(PZ * k, PZ * (k + 1))
            tr, ti = tw_ref[0, PZ * (g + k) : PZ * (g + k + 1), :], tw_ref[1, PZ * (g + k) : PZ * (g + k + 1), :]
            cols = []
            for side in sides:
                re, im = side[here, :LANES], side[here, LANES:]
                cols.append((re * tr + im * ti, im * tr - re * ti))
            back.append(cols)
    a = fft16([cols[0] for cols in back], 1)
    b = fft16([cols[1] for cols in back], 1)
    for p in range(0, PY, 4):
        stack = []
        for o in (p, p + 2):
            stack.append(jnp.concatenate([a[o][0], a[o][1], b[o][0], b[o][1], a[o + 1][0], a[o + 1][1], b[o + 1][0], b[o + 1][1]], axis=0))
        high, low = split(jnp.concatenate(stack, axis=1))
        part = mm(lh_ref[...], high) + mm(ll_ref[...], high) + mm(lh_ref[...], low)
        for o in range(4):
            at, lane = 64 * (o % 2), LANES * (o // 2)
            re, im = part[at : at + PZ, lane : lane + LANES], part[at + PZ : at + 64, lane : lane + LANES]
            out_ref[PZ * (p + o) : PZ * (p + o + 1), :] = re + pltpu.roll(im, OWN, 1)


def potential_kernel(in_ref, bh_ref, bl_ref, own_ref, edge_ref):
    for c in range(0, CH, 2):
        pots = []
        for h in range(2):
            high, low = split(in_ref[(c + h) * 64 : (c + h + 1) * 64, :].T)
            pot = mm(high, bh_ref[...]) + mm(high, bl_ref[...]) + mm(low, bh_ref[...])
            pot = pot[:OWN, :MESH] + pot[OWN:, MESH:]
            edge_ref[(c + h) * EDGE : (c + h + 1) * EDGE, :] = pot[:EDGE]
            pots.append(pot)
        high, low = split(jnp.concatenate(pots, axis=0))
        own_ref[c * OWN : (c + 2) * OWN, 0:MESH] = high
        own_ref[c * OWN : (c + 2) * OWN, MESH : 2 * MESH] = low


def read_back(pot_ref, w_ref, cells_ref, hit_ref, out_ref, layers, before):
    count = 8 * len(layers)
    group = 4 if count > 32 else CH
    for t in range(out_ref.shape[1] // TILE):
        lo = t * TILE
        slot = t % 2
        spread = atom_weights(w_ref, cells_ref, lo, layers)
        for k in range(4):
            hit = z_hits(cells_ref, lo, k)
            hit_ref[slot, 0:MESH, k * TILE : (k + 1) * TILE] = hit
            hit_ref[slot, MESH : 2 * MESH, k * TILE : (k + 1) * TILE] = hit
        for c in range(0, CH, group):
            near = mm(pot_ref[c * count : (c + group) * count, :], hit_ref[slot])
            for h in range(group):
                sums = [None] * 4
                for x, row in enumerate(spread):
                    for k in range(4):
                        r = h * count + 8 * x
                        term = row[k] * near[r : r + 8, k * TILE : (k + 1) * TILE]
                        sums[k] = term if x == 0 else sums[k] + term
                total = jnp.sum((sums[0] + sums[1]) + (sums[2] + sums[3]), axis=0, keepdims=True)
                if before is not None:
                    total = total + before[c + h : c + h + 1, lo : lo + TILE]
                out_ref[c + h : c + h + 1, lo : lo + TILE] = total


def own_kernel(pot_ref, w_ref, cells_ref, out_ref, hit_ref):
    read_back(pot_ref, w_ref, cells_ref, hit_ref, out_ref, range(BX), None)


def gather_kernel(edge_ref, before_ref, w_ref, cells_ref, out_ref, pot_ref, hit_ref):
    high, low = split(edge_ref[...])
    pot_ref[:, 0:MESH] = high
    pot_ref[:, MESH : 2 * MESH] = low
    read_back(pot_ref, w_ref, cells_ref, hit_ref, out_ref, range(BX, EX), before_ref)


def call(kernel, outs, scratch, flops, moved, *args, space=pltpu.VMEM, limit=40):
    shapes = [jax.ShapeDtypeStruct(*out) for out in outs]
    specs = [pl.BlockSpec(memory_space=pltpu.VMEM) for _ in outs]
    result = pl.pallas_call(
        kernel,
        out_shape=shapes,
        in_specs=[pl.BlockSpec(memory_space=space)] * len(args),
        out_specs=specs,
        scratch_shapes=scratch,
        compiler_params=pltpu.CompilerParams(vmem_limit_bytes=limit * 1024 * 1024),
        cost_estimate=pl.CostEstimate(flops=flops, bytes_accessed=moved, transcendentals=0),
    )(*args)
    return result[0] if len(outs) == 1 else result


def scatter(cotangent, spline_weights, base_cells):
    forth, _ = z_tables()
    table = np.stack(halves(forth))
    args = (cotangent, spline_weights, base_cells, table)
    scratch = [pltpu.VMEM(a.shape, a.dtype) for a in args] + [
        pltpu.VMEM((2, 4 * TILE, MESH), BF16),
        pltpu.VMEM((CH * ROWS, MESH), F32),
        pltpu.SemaphoreType.DMA((4,)),
    ]
    return call(scatter_kernel, [((CH * 128, LANES), F32)], scratch, 3 * 10**9, 10**6, *args, space=pltpu.HBM, limit=60)


def plane(blocks, filt):
    first, twist, second, third, last = plane_tables()
    return call(
        plane_kernel, [((PY * PZ, LANES), F32)], [], 10**9, 2 * 10**6,
        blocks, filt, *halves(first), twist, *halves(second), third, *halves(last),
    )


def potential(blocks):
    _, back = z_tables()
    outs = [((CH * OWN, 2 * MESH), BF16), ((CH * EDGE, MESH), F32)]
    return call(potential_kernel, outs, [], 10**9, 10**6, blocks, *halves(back))


def hits():
    return pltpu.VMEM((2, 2 * MESH, 4 * TILE), BF16)


def gather_own(own, spline_weights, base_cells):
    outs = [((CH, spline_weights.shape[1]), F32)]
    return call(own_kernel, outs, [hits()], 3 * 10**9, 10**6, own, spline_weights, base_cells)


def gather(edge, before, spline_weights, base_cells):
    scratch = [pltpu.VMEM((CH * EDGE, 2 * MESH), BF16), hits()]
    return call(gather_kernel, [(before.shape, F32)], scratch, 10**9, 10**6, edge, before, spline_weights, base_cells)


def filter_kernel(flag_ref, pair_ref, even_ref, pick_ref, out_ref):
    mine, other = [], []
    for p in range(PY):
        row = jnp.where(flag_ref[0] > 0, pair_ref[p, 1], pair_ref[p, 0])
        mine.append(row)
        other.append(jnp.where(flag_ref[1] > 0, even_ref[p], row))
    lane = lax.broadcasted_iota(jnp.int32, (PZ, LANES), 1) & 3
    for ab, rows in enumerate((other, mine)):
        rest = jnp.concatenate(rows, axis=0)
        parts = []
        for _ in range(3):
            part = rest.astype(BF16)
            rest = rest - part.astype(F32)
            parts.append(part)
        wide = mm(jnp.concatenate(parts, axis=0), pick_ref[...])
        wide = (wide[:MESH] + wide[MESH : 2 * MESH]) + wide[2 * MESH :]
        for k in range(PY):
            at = slice(LANES * k, LANES * (k + 1))
            value = wide[0:PZ, at]
            for n in range(1, 4):
                value = jnp.where(lane == n, wide[PZ * n : PZ * (n + 1), at], value)
            out_ref[PZ * k : PZ * (k + 1), LANES * ab : LANES * (ab + 1)] = value


def plane_filter(spectral_filter):
    p, q = lax.axis_index("py"), lax.axis_index("pz")
    half = PZ // 2
    pair = lax.all_to_all(spectral_filter.reshape(PY, 2, BX, MESH), "py", 0, 0)
    even = lax.ppermute(pair[:, 0], "pz", [(0, half)])
    flags = jnp.stack([q < half, (q == half) & (p % 2 == 0)]).astype(jnp.int32)
    pick = np.zeros((8, PY, PY, 4, 8, 4))
    for m in range(8):
        for k in range(PY):
            pick[m, k, k, :, m, :] = 1.0
    pick = pick.reshape(MESH, PY * LANES).astype(ml_dtypes.bfloat16)
    vmem = pl.BlockSpec(memory_space=pltpu.VMEM)
    return pl.pallas_call(
        filter_kernel,
        out_shape=jax.ShapeDtypeStruct((PY * PZ, 2 * LANES), F32),
        in_specs=[pl.BlockSpec(memory_space=pltpu.SMEM), vmem, vmem, vmem],
        out_specs=vmem,
        compiler_params=pltpu.CompilerParams(vmem_limit_bytes=32 * 1024 * 1024),
        cost_estimate=pl.CostEstimate(flops=10**9, bytes_accessed=10**6, transcendentals=0),
    )(flags, pair, even, pick)


def exchange(blocks):
    rows = blocks.shape[0] // (PY * PZ)
    return lax.all_to_all(blocks.reshape(PY * PZ, rows, LANES), ("py", "pz"), 0, 0).reshape(blocks.shape)


def on_device(cotangent, spline_weights, base_cells, spectral_filter):
    filt = plane_filter(spectral_filter)
    blocks = scatter(cotangent, spline_weights, base_cells)
    blocks = exchange(blocks)
    blocks = plane(blocks, filt)
    blocks = exchange(blocks)
    own, edge = potential(blocks)
    edge = lax.ppermute(edge, "py", [(p, (p - 1) % PY) for p in range(PY)])
    before = gather_own(own, spline_weights, base_cells)
    return gather(edge, before, spline_weights, base_cells)


def solution(mesh):
    return jax.shard_map(
        on_device,
        mesh=mesh,
        in_specs=(
            P(None, ("py", "pz")),
            P(None, ("py", "pz")),
            P(None, ("py", "pz")),
            P(None, "pz", "py", None),
        ),
        out_specs=P(None, ("py", "pz")),
        check_vma=False,
    )
```
